32 devices in a mesh: groups: 2 (over y), tm: 8 (over z, core), chan: 2 (over x), rows: 1.
Axes of the slice: x: 2, y: 2, z: 4, core: 2. Of those that a mesh axis runs over, the one named last changes fastest.
Arguments:
- video: bfloat16 [32, 8, 32, 512], P(('groups', 'tm'), 'rows', None, 'chan'), parts along dimension 0, may hold values from -6 to 6
- channel_gain: float32 [512], P('chan'), may hold values from 0.1 to 1.9
- weights: bfloat16 [27, 512, 512], P(None, None, 'chan'), may hold values from -0.0546875 to 0.0546875
- lengths: int32 [8], P('groups'), parts along dimension 0, may hold values from 1 to 8, 16 in all
- cotangent: bfloat16 [32, 8, 32, 512], P(('groups', 'tm'), 'rows', None, 'chan'), parts along dimension 0, may hold values from -6 to 6
Outputs:
- output: bfloat16 [32, 8, 32, 512], P(('groups', 'tm'), 'rows', None, 'chan'), parts along dimension 0
- input_grad: bfloat16 [32, 8, 32, 512], P(('groups', 'tm'), 'rows', None, 'chan'), parts along dimension 0
- weight_grad: float32 [54, 512, 512], P('groups', ('tm', 'rows'), 'chan'), parts along dimension 0
The draws below stay inside these ranges and needn't reach their ends.
There are 2 independent parts, one for each index of `groups`. The reference program is written for one: setup_inputs(seed, part) draws one part's arguments, and reference() takes and returns one part's arrays. A program takes and returns all parts, laid end to end along the dimension named above; an argument that names none is the same for every part. Nothing has to cross between parts.
Inputs may be any that keep to these rules, and one draw needn't show every extreme that they name: The 4 lengths sum to 16; the longest is exactly 8.
All inputs are finite; a program needn't handle non-finite values.
Results may differ from the reference program's by a relative error of at most 0.004.
Values may be sent and summed in bfloat16 or wider, within the bound.
A program may use at most 128 MiB of HBM per device.

```python
import math
import jax
import jax.numpy as jnp
import numpy as np
from jax import lax

C = 512
WID = 32
FRAMES = 16
HEIGHT = 8
CLIPS = 4
MOST = 8


def level_of(rng, dims, split, least, largest):
    factor_of, own = 1.0, jax.random.fold_in(rng, 6)
    for axis_at, blocks in split:
        draws = jnp.exp(jax.random.uniform(jax.random.fold_in(own, axis_at), (blocks,), jnp.float32, least / len(split), largest / len(split)))
        factor_of = factor_of * jnp.repeat(draws, dims[axis_at] // blocks).reshape([-1 if axis == axis_at else 1 for axis in range(len(dims))])
    return factor_of


def profile(count, total, most, slope):
    portions = [(1 << 20) // math.isqrt(rank ** slope) + 1 for rank in range(2, count + 1)]
    spare, counts = total - most - (count - 1), [1] * (count - 1)
    while spare > 0:
        candidates = [i for i in range(count - 1) if counts[i] < most]
        pool, budget = sum([portions[i] for i in candidates]), spare
        for i in candidates:
            addition = min(most - counts[i], max(1, budget * portions[i] // pool), spare)
            counts[i] = counts[i] + addition
            spare = spare - addition
    return np.array([most] + counts)


def ragged_sizes(own_key, amount, total, reach, slope):
    if amount == 2:
        one = jax.random.randint(own_key, (), max(1, total - reach), min(reach, total - 1) + 1)
        return jnp.stack([one, total - one])
    sizes = jnp.asarray(profile(amount, total, reach, slope), jnp.int32)
    twos = (amount - 1) // 2
    donor, sink = sizes[1:1 + 2 * twos:2], sizes[2:2 + 2 * twos:2]
    room = jnp.minimum(donor - 1, reach - sink)
    passed = jax.random.randint(jax.random.fold_in(own_key, 1), (twos,), 0, 1 << 20) % (room + 1)
    sizes = sizes.at[1:1 + 2 * twos:2].set(donor - passed).at[2:2 + 2 * twos:2].set(sink + passed)
    return sizes[jax.random.permutation(jax.random.fold_in(own_key, 2), amount)]


def scatter_about(key, shape, width, reach, shards=(), kind=jnp.bfloat16):
    gain = level_of(key, shape, shards, -0.22, 0.18) if shards else 1.0
    drawn = jax.random.normal(key, shape, jnp.float32) * width * gain
    return jnp.minimum(jnp.maximum(drawn, -reach), reach).astype(kind)


def setup_inputs(seed: int = 0, part: int = 0) -> dict:
    keys = jax.random.split(jax.random.key(seed), 6)
    own_keys = jax.random.split(jax.random.fold_in(keys[5], part), 6)
    return {
        "video": scatter_about(own_keys[0], (FRAMES, HEIGHT, WID, C), 1.0, 6.0, ((0, 8), (3, 2))),
        "channel_gain": jnp.clip(1.0 + 0.18 * jax.random.normal(keys[1], (C,), jnp.float32), 0.1, 1.9),
        "weights": scatter_about(keys[2], (27, C, C), (27 * C) ** -0.5, 0.0546875, ((2, 2),)),
        "lengths": ragged_sizes(own_keys[3], CLIPS, FRAMES, MOST, 0).astype(jnp.int32),
        "cotangent": scatter_about(own_keys[4], (FRAMES, HEIGHT, WID, C), 1.0, 6.0, ((0, 8), (3, 2))),
    }


def clip_tables(lengths, frame_ids):
    clip_lens = lengths.astype(jnp.int32)
    clip_ends = jnp.cumsum(clip_lens).astype(jnp.int32)
    clip_starts = (clip_ends - clip_lens).astype(jnp.int32)
    clip_ids = lax.optimization_barrier(jnp.sum((frame_ids[:, None] >= clip_ends[None, :]).astype(jnp.int32), axis=1)).astype(jnp.int32)
    clip_first = lax.optimization_barrier(jnp.max(jnp.where(clip_starts[None, :] <= frame_ids[:, None], clip_starts[None, :], 0), axis=1)).astype(jnp.int32)
    opening = jnp.any(clip_starts[None, :] == frame_ids[:, None], axis=1)
    return (clip_ids, clip_first, opening)

def reference(video, channel_gain, weights, lengths, cotangent):
    frame_count, row_count, col_count, all_chans = video.shape
    pixel_count = frame_count * row_count * col_count
    frame_ids = jnp.arange(frame_count + 2, dtype=jnp.int32)
    clip_ids, clip_first, opening = clip_tables(lengths, frame_ids)
    own_frames = frame_ids[:frame_count]
    scaled = video.astype(jnp.float32) * channel_gain
    activated = jax.nn.silu(scaled).astype(jnp.bfloat16)
    act_pad = jnp.pad(activated, ((0, 0), (1, 1), (1, 1), (0, 0)))
    grad_pad = jnp.pad(cotangent, ((0, 0), (1, 1), (1, 1), (0, 0)))
    flat_grad = cotangent.reshape(pixel_count, all_chans)
    output_sum = jnp.zeros((pixel_count, all_chans), jnp.float32)
    weight_terms = []
    lagged = []
    for lag_step in range(3):
        source = jnp.maximum(own_frames - lag_step, clip_first[:frame_count]).astype(jnp.int32)
        chosen = jnp.take(act_pad, source, axis=0)
        tap_stack = jnp.stack([chosen[:, row_step:row_step + row_count, col_step:col_step + col_count, :] for row_step in range(3) for col_step in range(3)], axis=3).reshape(pixel_count, 9 * all_chans)
        kernel = weights[9 * lag_step:9 * lag_step + 9].reshape(9 * all_chans, all_chans)
        output_sum = output_sum + jnp.dot(tap_stack, kernel, preferred_element_type=jnp.float32)
        weight_terms.append(lax.dot_general(tap_stack, flat_grad, (((0,), (0,)), ((), ())), preferred_element_type=jnp.float32).reshape(9, all_chans, all_chans))
        back_stack = jnp.stack([grad_pad[:, 2 - row_step:2 - row_step + row_count, 2 - col_step:2 - col_step + col_count, :] for row_step in range(3) for col_step in range(3)], axis=3).reshape(pixel_count, 9 * all_chans)
        back_kernel = jnp.transpose(weights[9 * lag_step:9 * lag_step + 9], (0, 2, 1)).reshape(9 * all_chans, all_chans)
        partial_value = jnp.dot(back_stack, back_kernel, preferred_element_type=jnp.float32).reshape(frame_count, row_count, col_count, all_chans)
        lagged.append(jnp.pad(partial_value, ((0, 2), (0, 0), (0, 0), (0, 0))))
    here_ids = clip_ids[:frame_count]
    start_flag = opening[:frame_count].astype(jnp.float32)
    act_grad = jnp.zeros((frame_count, row_count, col_count, all_chans), jnp.float32)
    for lag_step in range(3):
        same_clip = (clip_ids[lag_step:lag_step + frame_count] == here_ids).astype(jnp.float32)
        act_grad = act_grad + same_clip[:, None, None, None] * lagged[lag_step][lag_step:lag_step + frame_count]
        for inner_step in range(lag_step):
            near_clip = (clip_ids[inner_step:inner_step + frame_count] == here_ids).astype(jnp.float32) * start_flag
            act_grad = act_grad + near_clip[:, None, None, None] * lagged[lag_step][inner_step:inner_step + frame_count]
    output = (video.astype(jnp.float32) + output_sum.reshape(frame_count, row_count, col_count, all_chans)).astype(jnp.bfloat16)
    sigmoid_value = jax.nn.sigmoid(scaled)
    slope_factor = sigmoid_value * (1.0 + scaled * (1.0 - sigmoid_value))
    input_grad = (cotangent.astype(jnp.float32) + act_grad * slope_factor * channel_gain).astype(jnp.bfloat16)
    weight_grad = jnp.concatenate(weight_terms, axis=0) * (1.0 / math.sqrt(pixel_count))
    return (output, input_grad, weight_grad)
```

```python
import functools
import math

import jax
import jax.numpy as jnp
from jax import lax
from jax.experimental import pallas as pl
from jax.experimental.pallas import tpu as pltpu
from jax.sharding import PartitionSpec as P

MESH = pl.DeviceIdType.MESH
LAGS = 3
SIDE = 3
TAPS = SIDE * SIDE


def clip_tables(lengths, frame_ids):
    order = jnp.arange(lengths.shape[0], dtype=jnp.int32)
    clip_ends = jnp.sum(
        jnp.where(order[None, :] <= order[:, None], lengths[None, :], 0), axis=1
    ).astype(jnp.int32)
    clip_starts = clip_ends - lengths
    clip_ids = jnp.sum((frame_ids[:, None] >= clip_ends[None, :]).astype(jnp.int32), axis=1)
    clip_first = jnp.max(
        jnp.where(clip_starts[None, :] <= frame_ids[:, None], clip_starts[None, :], 0), axis=1
    )
    opening = jnp.any(clip_starts[None, :] == frame_ids[:, None], axis=1)
    return (clip_ids, clip_first, opening)


def kernel(
    dims,
    table_ref,
    coef_ref,
    act_ref,
    act_t_ref,
    cot_ref,
    w_ref,
    out_ref,
    grad_ref,
    wgrad_ref,
    x_prev,
    x_own,
    cots,
    act_ts,
    w_buf,
    pad_x,
    pad_g,
    stack,
    partial,
    p_out,
    p_in,
    w_sem,
    xp_send,
    xp_recv,
    xo_send,
    xo_recv,
    cot_send,
    cot_recv,
    at_send,
    at_recv,
    p_send,
    p_recv,
):
    n_tm, n_chan, n_rows, frames, height, width, own = dims
    t, c = lax.axis_index("tm"), lax.axis_index("chan")
    r = lax.axis_index("rows") if n_rows > 1 else 0
    pixels = n_rows * height * width
    local = height * width
    block = act_ts.shape[1]
    pair = 2 if n_tm % 2 == 0 else 1
    side, place, places = t % pair, t // pair, n_tm // pair
    sibling = t + 1 - 2 * side

    load_w = pltpu.make_async_copy(w_ref, w_buf, w_sem)
    load_w.start()

    barrier = pltpu.get_barrier_semaphore()
    for tt in range(n_tm):
        for cc in range(n_chan):

            @pl.when((tt != t) | (cc != c))
            def _():
                pl.semaphore_signal(
                    barrier, inc=1, device_id={"tm": tt, "chan": cc}, device_id_type=MESH
                )

    x_own[c] = act_ref[...]
    cots[t] = cot_ref[...]
    pl.semaphore_wait(barrier, n_tm * n_chan - 1)

    def send_own(cc):
        return pltpu.make_async_remote_copy(
            act_ref, x_own.at[c], xo_send.at[cc], xo_recv.at[c],
            device_id={"chan": cc}, device_id_type=MESH,
        )

    def send_prev(cc):
        return pltpu.make_async_remote_copy(
            act_ref.at[pl.ds((frames - 2) * pixels, 2 * pixels)], x_prev.at[c],
            xp_send.at[cc], xp_recv.at[c],
            device_id={"tm": t + 1, "chan": cc}, device_id_type=MESH,
        )

    def send_cot(s, way, to):
        return pltpu.make_async_remote_copy(
            cots.at[s], cots.at[s], cot_send.at[way, s], cot_recv.at[s],
            device_id={"tm": to}, device_id_type=MESH,
        )

    def send_at(tt, cc):
        row = (tt * n_rows + r) * block - c * own
        if n_rows > 1:
            row = pl.multiple_of(row, 16)
        return pltpu.make_async_remote_copy(
            act_t_ref.at[pl.ds(row, block)], act_ts.at[t], at_send.at[tt, cc], at_recv.at[t],
            device_id={"tm": tt, "chan": cc}, device_id_type=MESH,
        )

    def for_at(act):
        for step in range(n_tm):
            for cc in range(n_chan):
                tt = step
                mine = ((tt * n_rows + r) * block) // own == c

                @pl.when(mine & ((tt != t) | (cc != c)))
                def _():
                    act(tt, cc)

    def arrived(ref, sem):
        pltpu.make_async_remote_copy(
            ref, ref, sem, sem, device_id={"tm": t}, device_id_type=MESH
        ).wait_recv()

    def cot_moves(s, from_left, act):
        if from_left is not False:

            @pl.when(place + 1 < places)
            def _():
                act(s, 0, t + pair)

        if from_left is not True:

            @pl.when(place > 0)
            def _():
                act(s, 1, t - pair)

        if pair == 2:
            act(s, 2, sibling)

    def start_cot(s, way, to):
        send_cot(s, way, to).start()

    def finish_cot(s, way, to):
        send_cot(s, way, to).wait_send()

    def hop(d):
        @pl.when(place - d >= 0)
        def _():
            s = t - pair * d
            arrived(cots.at[s], cot_recv.at[s])
            cot_moves(s, True, start_cot)

        @pl.when(place + d < places)
        def _():
            s = t + pair * d
            arrived(cots.at[s], cot_recv.at[s])
            cot_moves(s, False, start_cot)

    cot_moves(t, None, start_cot)
    for cc in range(n_chan):

        @pl.when(cc != c)
        def _():
            send_own(cc).start()

        @pl.when(t + 1 < n_tm)
        def _():
            send_prev(cc).start()

    for_at(lambda tt, cc: send_at(tt, cc).start())
    row0 = (t * n_rows + r) * block

    @pl.when(row0 // own == c)
    def _():
        act_ts[t] = act_t_ref[pl.ds(pl.multiple_of(row0 - c * own, 16), block), :]

    column = lax.broadcasted_iota(jnp.int32, (pixels, 1), 0) % width

    def columns(value, step):
        if step == 0:
            return value
        moved = pltpu.roll(value, (-step) % pixels, axis=0)
        return jnp.where((column + step >= 0) & (column + step < width), moved, 0.0)

    edge = (n_rows * height + 1) * width

    def fill(ref, value, sign):
        for b in range(SIDE):
            ref[b, pl.ds(width, pixels), :] = columns(value, sign * (b - 1)).astype(jnp.bfloat16)

    pad_x[:, :, :width, :] = jnp.zeros_like(pad_x[:, :, :width, :])
    pad_x[:, :, edge:, :] = jnp.zeros_like(pad_x[:, :, edge:, :])
    pad_g[:, :, :, :width, :] = jnp.zeros_like(pad_g[:, :, :, :width, :])
    pad_g[:, :, :, edge:, :] = jnp.zeros_like(pad_g[:, :, :, edge:, :])
    partial[...] = jnp.zeros_like(partial)
    out_ref[...] = jnp.zeros_like(out_ref)
    wgrad_ref[...] = jnp.zeros_like(wgrad_ref)

    if places > 1:
        hop(1)

    if pair == 2:

        @pl.when(side == 0)
        def _():
            arrived(cots.at[sibling], cot_recv.at[sibling])

        @pl.when((side == 1) & (t + 1 < n_tm))
        def _():
            arrived(cots.at[t + 1], cot_recv.at[t + 1])

    def cot_frame(f):
        frame = jnp.minimum(t * frames + f, n_tm * frames - 1)
        return cots[frame // frames, pl.ds((frame % frames) * pixels, pixels), :].astype(jnp.float32)

    for f in range(frames):
        near = [cot_frame(f + m) for m in range(LAGS)]
        for lag in range(LAGS):
            mixed = sum(coef_ref[(f * LAGS + lag) * LAGS + m] * near[m] for m in range(lag + 1))
            fill(pad_g.at[f, lag], mixed, -1)

    load_w.wait()

    def back(k, _):
        lag, a, b = k // TAPS, (k % TAPS) // SIDE, k % SIDE
        start = pl.multiple_of((r * height + 2 - a) * width, 16)
        grads = jnp.concatenate(
            [pad_g[f, lag, b, pl.ds(start, local), :] for f in range(frames)], axis=0
        )
        partial[...] += lax.dot_general(
            grads, w_buf[k], (((1,), (1,)), ((), ())), preferred_element_type=jnp.float32
        )
        return 0

    lax.fori_loop(0, LAGS * TAPS, back, 0)

    def send_p(cc):
        return pltpu.make_async_remote_copy(
            p_out.at[cc], p_in.at[c], p_send.at[cc], p_recv.at[c],
            device_id={"chan": cc}, device_id_type=MESH,
        )

    for cc in range(n_chan):

        @pl.when(cc != c)
        def _():
            p_out[cc] = partial[:, cc * own : (cc + 1) * own].astype(jnp.bfloat16)
            send_p(cc).start()

    if places > 2:
        hop(2)

    for cc in range(n_chan):

        @pl.when(cc != c)
        def _():
            arrived(x_own.at[cc], xo_recv.at[cc])

        @pl.when(t > 0)
        def _():
            arrived(x_prev.at[cc], xp_recv.at[cc])

    for cc in range(n_chan):
        for slot in range(2 + frames):
            if slot < 2:
                value = x_prev[cc, slot * pixels : (slot + 1) * pixels, :]
            else:
                value = x_own[cc, (slot - 2) * pixels : (slot - 1) * pixels, :]
            fill(
                pad_x.at[slot, :, :, cc * own : (cc + 1) * own], value.astype(jnp.float32), 1
            )

    if places > 3:
        hop(3)

    def ahead(k, _):
        lag, a, b = k // TAPS, (k % TAPS) // SIDE, k % SIDE
        start = pl.multiple_of((r * height + a) * width, 16)
        taps = jnp.concatenate(
            [
                pad_x[table_ref[f * LAGS + lag], b, pl.ds(start, local), :]
                for f in range(frames)
            ],
            axis=0,
        )
        out_ref[...] += jnp.dot(taps, w_buf[k], preferred_element_type=jnp.float32)
        return 0

    lax.fori_loop(0, LAGS * TAPS, ahead, 0)

    for d in range(4, places):
        hop(d)

    place_of = lax.broadcasted_iota(jnp.int32, (1, pixels), 1)
    line, spot = place_of // width, place_of % width

    for_owner = row0 // own != c

    def build(s, _):
        @pl.when((s != t) | for_owner)
        def _():
            arrived(act_ts.at[s], at_recv.at[s])

        for f in range(frames):
            value = act_ts[s, :, f * pixels : (f + 1) * pixels].astype(jnp.float32)
            for k in range(TAPS):
                down, right = k // SIDE - 1, k % SIDE - 1
                step = down * width + right
                moved = value if step == 0 else pltpu.roll(value, (-step) % pixels, axis=1)
                inside = (
                    (line + down >= 0)
                    & (line + down < n_rows * height)
                    & (spot + right >= 0)
                    & (spot + right < width)
                )
                stack[s * frames + f, k * block : (k + 1) * block, :] = jnp.where(
                    inside, moved, 0.0
                ).astype(jnp.bfloat16)
        return 0

    lax.fori_loop(0, n_tm, build, 0)

    if pair == 2:
        for q in range(places):
            s = q * pair + 1 - side
            early = ((side == 0) & (s == sibling)) | ((side == 1) & (s == t + 1))

            @pl.when(jnp.logical_not(early))
            def _():
                arrived(cots.at[s], cot_recv.at[s])

    def weigh(s, _):
        for lag in range(LAGS):
            taps = jnp.concatenate(
                [
                    stack[table_ref[frames * LAGS + (s * frames + f) * LAGS + lag]]
                    for f in range(frames)
                ],
                axis=1,
            )
            rows = pl.ds(lag * TAPS * block, TAPS * block)
            wgrad_ref[rows, :] += jnp.dot(taps, cots[s], preferred_element_type=jnp.float32)
        return 0

    lax.fori_loop(0, n_tm, weigh, 0)

    total = partial[:, pl.ds(pl.multiple_of(c * own, 128), own)]
    grad_ref[...] = total
    for cc in range(n_chan):

        @pl.when(cc != c)
        def _():
            arrived(p_in.at[cc], p_recv.at[cc])
            grad_ref[...] += p_in[cc].astype(jnp.float32)
            send_p(cc).wait_send()
            send_own(cc).wait_send()

        @pl.when(t + 1 < n_tm)
        def _():
            send_prev(cc).wait_send()

    for_at(lambda tt, cc: send_at(tt, cc).wait_send())
    cot_moves(t, None, finish_cot)
    for d in range(1, places):

        @pl.when(place - d >= 0)
        def _():
            cot_moves(t - pair * d, True, finish_cot)

        @pl.when(place + d < places)
        def _():
            cot_moves(t + pair * d, False, finish_cot)


def shards(video, channel_gain, weights, lengths, cotangent):
    frame_count, row_count, col_count, own = video.shape
    taps, all_chans, _ = weights.shape
    n_tm, n_chan, n_rows = (lax.axis_size(a) for a in ("tm", "chan", "rows"))
    local_count = frame_count * row_count * col_count
    total_pixels = local_count * n_tm * n_rows
    all_frames = n_tm * frame_count
    block = all_chans // (n_tm * n_rows)
    frame_base = lax.axis_index("tm") * frame_count
    frame_ids = jnp.arange(all_frames + 2, dtype=jnp.int32)
    clip_ids, clip_first, opening = clip_tables(lengths, frame_ids)
    lags = jnp.arange(LAGS, dtype=jnp.int32)
    sources = jnp.maximum(frame_ids[:all_frames, None] - lags, clip_first[:all_frames, None])
    mine = lax.dynamic_slice_in_dim(sources, frame_base, frame_count, 0)
    table = jnp.concatenate([(mine - frame_base + 2).reshape(-1), sources.reshape(-1)])
    ids = lax.dynamic_slice_in_dim(clip_ids, frame_base, frame_count + 2, 0)
    opens = lax.dynamic_slice_in_dim(opening, frame_base, frame_count, 0)
    same = jnp.stack([ids[m : m + frame_count] == ids[:frame_count] for m in range(LAGS)], axis=1)
    coef = jnp.where(
        lags[None, :, None] == lags[None, None, :],
        same[:, None, :],
        (lags[None, None, :] < lags[None, :, None]) & same[:, None, :] & opens[:, None, None],
    ).astype(jnp.float32).reshape(-1)

    scaled = video.astype(jnp.float32) * channel_gain
    activated = jax.nn.silu(scaled).astype(jnp.bfloat16)
    act_full, cot_full = activated, cotangent
    if n_rows > 1:
        act_full = lax.all_gather(activated, "rows", axis=1, tiled=True)
        cot_full = lax.all_gather(cotangent, "rows", axis=1, tiled=True)
    act_full = act_full.reshape(-1, own)
    cot_full = cot_full.reshape(-1, own)
    act_t = act_full.T

    full = act_full.shape[0]
    pixels = full // frame_count
    padded = pixels + 2 * col_count
    vmem = pl.BlockSpec(memory_space=pltpu.VMEM)
    smem = pl.BlockSpec(memory_space=pltpu.SMEM)
    bf16, f32 = jnp.bfloat16, jnp.float32
    dma = pltpu.SemaphoreType.DMA
    out_sum, act_grad, weight_sum = pl.pallas_call(
        functools.partial(
            kernel, (n_tm, n_chan, n_rows, frame_count, row_count, col_count, own)
        ),
        out_shape=(
            jax.ShapeDtypeStruct((local_count, own), f32),
            jax.ShapeDtypeStruct((local_count, own), f32),
            jax.ShapeDtypeStruct((taps * block, own), f32),
        ),
        in_specs=[smem, smem, vmem, vmem, vmem, pl.BlockSpec(memory_space=pl.ANY)],
        out_specs=(vmem, vmem, vmem),
        scratch_shapes=[
            pltpu.VMEM((n_chan, 2 * pixels, own), bf16),
            pltpu.VMEM((n_chan, full, own), bf16),
            pltpu.VMEM((n_tm, full, own), bf16),
            pltpu.VMEM((n_tm, block, full), bf16),
            pltpu.VMEM(weights.shape, bf16),
            pltpu.VMEM((2 + frame_count, SIDE, padded, all_chans), bf16),
            pltpu.VMEM((frame_count, LAGS, SIDE, padded, own), bf16),
            pltpu.VMEM((all_frames, TAPS * block, pixels), bf16),
            pltpu.VMEM((local_count, all_chans), f32),
            pltpu.VMEM((n_chan, local_count, own), bf16),
            pltpu.VMEM((n_chan, local_count, own), bf16),
            dma,
            dma((n_chan,)),
            dma((n_chan,)),
            dma((n_chan,)),
            dma((n_chan,)),
            dma((3, n_tm)),
            dma((n_tm,)),
            dma((n_tm, n_chan)),
            dma((n_tm,)),
            dma((n_chan,)),
            dma((n_chan,)),
        ],
        compiler_params=pltpu.CompilerParams(
            collective_id=0, has_side_effects=True, vmem_limit_bytes=56 * 2**20
        ),
        cost_estimate=pl.CostEstimate(
            flops=6 * local_count * taps * all_chans * own,
            bytes_accessed=2 * weights.size + 4 * taps * block * own,
            transcendentals=0,
        ),
    )(table, coef, act_full, act_t, cot_full, weights)

    output = (video.astype(f32) + out_sum.reshape(video.shape)).astype(bf16)
    sigmoid_value = jax.nn.sigmoid(scaled)
    slope_factor = sigmoid_value * (1.0 + scaled * (1.0 - sigmoid_value))
    input_grad = (
        cotangent.astype(f32) + act_grad.reshape(video.shape) * slope_factor * channel_gain
    ).astype(bf16)
    weight_grad = weight_sum.reshape(taps, block, own) * (1.0 / math.sqrt(total_pixels))
    return (output, input_grad, weight_grad)


def solution(mesh):
    in_specs = (
        P(("groups", "tm"), "rows", None, "chan"),
        P("chan"),
        P(None, None, "chan"),
        P("groups"),
        P(("groups", "tm"), "rows", None, "chan"),
    )
    out_specs = (
        P(("groups", "tm"), "rows", None, "chan"),
        P(("groups", "tm"), "rows", None, "chan"),
        P("groups", ("tm", "rows"), "chan"),
    )
    return jax.shard_map(shards, mesh=mesh, in_specs=in_specs, out_specs=out_specs, check_vma=False)
```

```python
import functools
import math

import jax
import jax.numpy as jnp
from jax import lax
from jax.experimental import pallas as pl
from jax.experimental.pallas import tpu as pltpu
from jax.sharding import PartitionSpec as P

MESH = pl.DeviceIdType.MESH
LAGS = 3
SIDE = 3
TAPS = SIDE * SIDE


def kernel(
    dims,
    lengths_ref,
    video_ref,
    gain_ref,
    cot_ref,
    w_ref,
    out_ref,
    grad_ref,
    wgrad_ref,
    table_ref,
    act_t_ref,
    x_prev,
    x_own,
    cots,
    act_ts,
    w_buf,
    pad_x,
    pad_g,
    stack,
    partial,
    p_out,
    p_in,
    w_sem,
    xp_send,
    xr_send,
    xp_recv,
    xo_send,
    xo_recv,
    cot_send,
    cot_recv,
    at_send,
    at_recv,
    p_send,
    p_recv,
):
    n_tm, n_chan, n_rows, frames, height, width, own = dims
    t, c = lax.axis_index("tm"), lax.axis_index("chan")
    r = lax.axis_index("rows") if n_rows > 1 else 0
    pixels = n_rows * height * width
    local = height * width
    block = act_ts.shape[1]
    pair = 2 if n_tm % 2 == 0 else 1
    side, place, places = t % pair, t // pair, n_tm // pair
    sibling = t + 1 - 2 * side

    load_w = pltpu.make_async_copy(w_ref, w_buf, w_sem)
    load_w.start()

    barrier = pltpu.get_barrier_semaphore()
    for tt in range(n_tm):
        for cc in range(n_chan):

            @pl.when((tt != t) | (cc != c))
            def _():
                pl.semaphore_signal(
                    barrier, inc=1, device_id={"tm": tt, "chan": cc}, device_id_type=MESH
                )

    gain = gain_ref[...]
    for f in range(frames):
        rows = slice(f * pixels, (f + 1) * pixels)
        scaled = video_ref[rows, :].astype(jnp.float32) * gain
        acted = (scaled / (1.0 + jnp.exp(-scaled))).astype(jnp.bfloat16)
        x_own[c, rows, :] = acted
        act_t_ref[:, rows] = acted.astype(jnp.float32).T.astype(jnp.bfloat16)
    cots[t] = cot_ref[...]

    starts, begun = [], jnp.int32(0)
    for clip in range(lengths_ref.shape[0]):
        starts.append(begun)
        begun = begun + lengths_ref[clip]

    def first_of(frame):
        value = jnp.int32(0)
        for begun_at in starts[1:]:
            value = jnp.where(begun_at <= frame, begun_at, value)
        return jnp.where(frame >= begun, begun, value)

    def note(frame, _):
        first = first_of(frame)
        for lag in range(LAGS):
            table_ref[frame * LAGS + lag] = jnp.maximum(frame - lag, first)
        return 0

    lax.fori_loop(0, n_tm * frames, note, 0)

    def send_own(cc):
        return pltpu.make_async_remote_copy(
            x_own.at[c], x_own.at[c], xo_send.at[cc], xo_recv.at[c],
            device_id={"chan": cc}, device_id_type=MESH,
        )

    def send_prev():
        return pltpu.make_async_remote_copy(
            x_own.at[c, pl.ds((frames - 2) * pixels, 2 * pixels)], x_prev.at[c],
            xp_send.at[c], xp_recv.at[c],
            device_id={"tm": t + 1}, device_id_type=MESH,
        )

    def pass_prev(cc):
        return pltpu.make_async_remote_copy(
            x_prev.at[c], x_prev.at[c], xr_send.at[cc], xp_recv.at[c],
            device_id={"chan": cc}, device_id_type=MESH,
        )

    def send_cot(s, way, to):
        return pltpu.make_async_remote_copy(
            cots.at[s], cots.at[s], cot_send.at[way, s], cot_recv.at[s],
            device_id={"tm": to}, device_id_type=MESH,
        )

    def send_at(tt, cc):
        row = pl.multiple_of((tt * n_rows + r) * block - c * own, 16)
        return pltpu.make_async_remote_copy(
            act_t_ref.at[pl.ds(row, block)], act_ts.at[t], at_send.at[tt, cc], at_recv.at[t],
            device_id={"tm": tt, "chan": cc}, device_id_type=MESH,
        )

    def for_at(act):
        for step in range(n_tm):
            for cc in range(n_chan):
                tt = step
                mine = ((tt * n_rows + r) * block) // own == c

                @pl.when(mine & ((tt != t) | (cc != c)))
                def _():
                    act(tt, cc)

    def arrived(ref, sem):
        pltpu.make_async_remote_copy(
            ref, ref, sem, sem, device_id={"tm": t}, device_id_type=MESH
        ).wait_recv()

    def cot_moves(s, from_left, act):
        if from_left is not False:

            @pl.when(place + 1 < places)
            def _():
                act(s, 0, t + pair)

        if from_left is not True:

            @pl.when(place > 0)
            def _():
                act(s, 1, t - pair)

        if pair == 2:
            act(s, 2, sibling)

    def start_cot(s, way, to):
        send_cot(s, way, to).start()

    def finish_cot(s, way, to):
        send_cot(s, way, to).wait_send()

    def hop(d):
        @pl.when(place - d >= 0)
        def _():
            s = t - pair * d
            arrived(cots.at[s], cot_recv.at[s])
            cot_moves(s, True, start_cot)

        @pl.when(place + d < places)
        def _():
            s = t + pair * d
            arrived(cots.at[s], cot_recv.at[s])
            cot_moves(s, False, start_cot)

    row0 = (t * n_rows + r) * block
    for_owner = row0 // own != c

    @pl.when(jnp.logical_not(for_owner))
    def _():
        act_ts[t] = act_t_ref[pl.ds(pl.multiple_of(row0 - c * own, 16), block), :]

    column = lax.broadcasted_iota(jnp.int32, (pixels, 1), 0) % width

    def columns(value, step):
        if step == 0:
            return value
        moved = pltpu.roll(value, (-step) % pixels, axis=0)
        return jnp.where((column + step >= 0) & (column + step < width), moved, 0.0)

    edge = (n_rows * height + 1) * width

    def fill(ref, value, sign):
        for b in range(SIDE):
            ref[b, pl.ds(width, pixels), :] = columns(value, sign * (b - 1)).astype(jnp.bfloat16)

    pad_x[:, :, :width, :] = jnp.zeros_like(pad_x[:, :, :width, :])
    pad_x[:, :, edge:, :] = jnp.zeros_like(pad_x[:, :, edge:, :])
    pad_g[:, :, :, :width, :] = jnp.zeros_like(pad_g[:, :, :, :width, :])
    pad_g[:, :, :, edge:, :] = jnp.zeros_like(pad_g[:, :, :, edge:, :])

    def fill_own(cc):
        for f in range(frames):
            value = x_own[cc, f * pixels : (f + 1) * pixels, :].astype(jnp.float32)
            lanes = pl.ds(pl.multiple_of(cc * own, 128), own)
            fill(pad_x.at[2 + f, :, :, lanes], value, 1)

    def cot_frame(f):
        frame = jnp.minimum(t * frames + f, n_tm * frames - 1)
        rows = pl.ds(pl.multiple_of((frame % frames) * pixels, 16), pixels)
        return cots[frame // frames, rows, :].astype(jnp.float32)

    for f in range(frames):
        fill(pad_g.at[f, 0], cot_ref[f * pixels : (f + 1) * pixels, :].astype(jnp.float32), -1)
    fill_own(c)

    pl.semaphore_wait(barrier, n_tm * n_chan - 1)
    cot_moves(t, None, start_cot)
    for cc in range(n_chan):

        @pl.when(cc != c)
        def _():
            send_own(cc).start()

    @pl.when(t + 1 < n_tm)
    def _():
        send_prev().start()

    load_w.wait()

    def back(lag):
        for a in range(SIDE):
            start = pl.multiple_of((r * height + 2 - a) * width, 16)
            grads = jnp.concatenate(
                [
                    jnp.concatenate(
                        [pad_g[f, lag, b, pl.ds(start, local), :] for b in range(SIDE)], axis=1
                    )
                    for f in range(frames)
                ],
                axis=0,
            )
            k = lag * TAPS + a * SIDE
            kernels = jnp.concatenate([w_buf[k + b] for b in range(SIDE)], axis=1)
            found = lax.dot_general(
                grads, kernels, (((1,), (1,)), ((), ())), preferred_element_type=jnp.float32
            )
            if lag == 0 and a == 0:
                partial[...] = found
            else:
                partial[...] += found

    def ahead(lag):
        for a in range(SIDE):
            start = pl.multiple_of((r * height + a) * width, 16)

            def taps_of(f):
                slot = table_ref[t * frames * LAGS + f * LAGS + lag] - t * frames + 2
                return jnp.concatenate(
                    [pad_x[slot, b, pl.ds(start, local), :] for b in range(SIDE)], axis=1
                )

            taps = jnp.concatenate([taps_of(f) for f in range(frames)], axis=0)
            k = lag * TAPS + a * SIDE
            kernels = w_buf[k : k + SIDE].reshape(-1, own)
            found = jnp.dot(taps, kernels, preferred_element_type=jnp.float32)
            if lag == 0 and a == 0:
                out_ref[...] = found
            else:
                out_ref[...] += found

    def send_p(cc):
        return pltpu.make_async_remote_copy(
            p_out.at[cc], p_in.at[c], p_send.at[cc], p_recv.at[c],
            device_id={"chan": cc}, device_id_type=MESH,
        )

    hops = iter(range(1, places))

    def advance():
        for d in hops:
            hop(d)
            break

    back(0)
    advance()
    for_at(lambda tt, cc: send_at(tt, cc).start())
    for cc in range(n_chan):

        @pl.when(cc != c)
        def _():
            arrived(x_own.at[cc], xo_recv.at[cc])
            fill_own(cc)

    ahead(0)
    advance()

    @pl.when(t > 0)
    def _():
        arrived(x_prev.at[c], xp_recv.at[c])
        for cc in range(n_chan):

            @pl.when(cc != c)
            def _():
                pass_prev(cc).start()

    if pair == 2:

        @pl.when(side == 0)
        def _():
            arrived(cots.at[sibling], cot_recv.at[sibling])

        @pl.when((side == 1) & (t + 1 < n_tm))
        def _():
            arrived(cots.at[t + 1], cot_recv.at[t + 1])

    for f in range(frames):
        here = t * frames + f
        opens = first_of(here) == here
        near = [cot_frame(f + m) for m in range(LAGS)]
        same = [(first_of(here + m) == first_of(here)) & (here + m < begun) for m in range(LAGS)]
        for lag in range(1, LAGS):
            mixed = jnp.where(same[lag], near[lag], 0.0)
            for m in range(lag):
                mixed = mixed + jnp.where(same[m] & opens, near[m], 0.0)
            fill(pad_g.at[f, lag], mixed, -1)

    back(1)
    advance()
    back(2)
    for cc in range(n_chan):

        @pl.when(cc != c)
        def _():
            p_out[cc] = partial[:, cc * own : (cc + 1) * own].astype(jnp.bfloat16)
            send_p(cc).start()

    advance()
    for cc in range(n_chan):

        @pl.when((t > 0) & (cc != c))
        def _():
            arrived(x_prev.at[cc], xp_recv.at[cc])

        for slot in range(2):
            value = x_prev[cc, slot * pixels : (slot + 1) * pixels, :].astype(jnp.float32)
            fill(pad_x.at[slot, :, :, cc * own : (cc + 1) * own], value, 1)

    ahead(1)
    advance()
    ahead(2)
    for d in hops:
        hop(d)

    place_of = lax.broadcasted_iota(jnp.int32, (1, pixels), 1)
    line, spot = place_of // width, place_of % width

    def build(s, _):
        @pl.when((s != t) | for_owner)
        def _():
            arrived(act_ts.at[s], at_recv.at[s])

        for f in range(frames):
            value = act_ts[s, :, f * pixels : (f + 1) * pixels].astype(jnp.float32)
            for k in range(TAPS):
                down, right = k // SIDE - 1, k % SIDE - 1
                step = down * width + right
                moved = value if step == 0 else pltpu.roll(value, (-step) % pixels, axis=1)
                inside = (
                    (line + down >= 0)
                    & (line + down < n_rows * height)
                    & (spot + right >= 0)
                    & (spot + right < width)
                )
                stack[s * frames + f, k * block : (k + 1) * block, :] = jnp.where(
                    inside, moved, 0.0
                ).astype(jnp.bfloat16)
        return 0

    lax.fori_loop(0, n_tm, build, 0)

    if pair == 2:
        for q in range(places):
            s = q * pair + 1 - side
            early = ((side == 0) & (s == sibling)) | ((side == 1) & (s == t + 1))

            @pl.when(jnp.logical_not(early))
            def _():
                arrived(cots.at[s], cot_recv.at[s])

    def weigh(s, _):
        for lag in range(LAGS):
            taps = jnp.concatenate(
                [
                    stack[table_ref[(s * frames + f) * LAGS + lag]]
                    for f in range(frames)
                ],
                axis=1,
            )
            rows = pl.ds(lag * TAPS * block, TAPS * block)
            wgrad_ref[rows, :] += jnp.dot(taps, cots[s], preferred_element_type=jnp.float32)
        return 0

    wgrad_ref[...] = jnp.zeros_like(wgrad_ref)
    lax.fori_loop(0, n_tm, weigh, 0)

    total = partial[:, pl.ds(pl.multiple_of(c * own, 128), own)]
    grad_ref[...] = total
    for cc in range(n_chan):

        @pl.when(cc != c)
        def _():
            arrived(p_in.at[cc], p_recv.at[cc])
            grad_ref[...] += p_in[cc].astype(jnp.float32)
            send_p(cc).wait_send()
            send_own(cc).wait_send()

        @pl.when((t > 0) & (cc != c))
        def _():
            pass_prev(cc).wait_send()

    @pl.when(t + 1 < n_tm)
    def _():
        send_prev().wait_send()

    for_at(lambda tt, cc: send_at(tt, cc).wait_send())
    cot_moves(t, None, finish_cot)
    for d in range(1, places):

        @pl.when(place - d >= 0)
        def _():
            cot_moves(t - pair * d, True, finish_cot)

        @pl.when(place + d < places)
        def _():
            cot_moves(t + pair * d, False, finish_cot)


def shards(video, channel_gain, weights, lengths, cotangent):
    frame_count, row_count, col_count, own = video.shape
    taps, all_chans, _ = weights.shape
    n_tm, n_chan, n_rows = (lax.axis_size(a) for a in ("tm", "chan", "rows"))
    local_count = frame_count * row_count * col_count
    total_pixels = local_count * n_tm * n_rows
    all_frames = n_tm * frame_count
    block = all_chans // (n_tm * n_rows)
    scaled = video.astype(jnp.float32) * channel_gain
    video_full, cot_full = video, cotangent
    if n_rows > 1:
        video_full = lax.all_gather(video, "rows", axis=1, tiled=True)
        cot_full = lax.all_gather(cotangent, "rows", axis=1, tiled=True)
    video_full = video_full.reshape(-1, own)
    cot_full = cot_full.reshape(-1, own)

    full = video_full.shape[0]
    pixels = full // frame_count
    padded = pixels + 2 * col_count
    vmem = pl.BlockSpec(memory_space=pltpu.VMEM)
    smem = pl.BlockSpec(memory_space=pltpu.SMEM)
    bf16, f32 = jnp.bfloat16, jnp.float32
    dma = pltpu.SemaphoreType.DMA
    out_sum, act_grad, weight_sum = pl.pallas_call(
        functools.partial(
            kernel, (n_tm, n_chan, n_rows, frame_count, row_count, col_count, own)
        ),
        out_shape=(
            jax.ShapeDtypeStruct((local_count, own), f32),
            jax.ShapeDtypeStruct((local_count, own), f32),
            jax.ShapeDtypeStruct((taps * block, own), f32),
        ),
        in_specs=[smem, vmem, vmem, vmem, pl.BlockSpec(memory_space=pl.ANY)],
        out_specs=(vmem, vmem, vmem),
        scratch_shapes=[
            pltpu.SMEM((all_frames * LAGS,), jnp.int32),
            pltpu.VMEM((own, full), bf16),
            pltpu.VMEM((n_chan, 2 * pixels, own), bf16),
            pltpu.VMEM((n_chan, full, own), bf16),
            pltpu.VMEM((n_tm, full, own), bf16),
            pltpu.VMEM((n_tm, block, full), bf16),
            pltpu.VMEM(weights.shape, bf16),
            pltpu.VMEM((2 + frame_count, SIDE, padded, all_chans), bf16),
            pltpu.VMEM((frame_count, LAGS, SIDE, padded, own), bf16),
            pltpu.VMEM((all_frames, TAPS * block, pixels), bf16),
            pltpu.VMEM((local_count, all_chans), f32),
            pltpu.VMEM((n_chan, local_count, own), bf16),
            pltpu.VMEM((n_chan, local_count, own), bf16),
            dma,
            dma((n_chan,)),
            dma((n_chan,)),
            dma((n_chan,)),
            dma((n_chan,)),
            dma((n_chan,)),
            dma((3, n_tm)),
            dma((n_tm,)),
            dma((n_tm, n_chan)),
            dma((n_tm,)),
            dma((n_chan,)),
            dma((n_chan,)),
        ],
        compiler_params=pltpu.CompilerParams(
            collective_id=0, has_side_effects=True, vmem_limit_bytes=56 * 2**20
        ),
        cost_estimate=pl.CostEstimate(
            flops=6 * local_count * taps * all_chans * own,
            bytes_accessed=2 * weights.size + 4 * taps * block * own,
            transcendentals=0,
        ),
    )(lengths, video_full, channel_gain.reshape(1, own), cot_full, weights)

    output = (video.astype(f32) + out_sum.reshape(video.shape)).astype(bf16)
    sigmoid_value = jax.nn.sigmoid(scaled)
    slope_factor = sigmoid_value * (1.0 + scaled * (1.0 - sigmoid_value))
    input_grad = (
        cotangent.astype(f32) + act_grad.reshape(video.shape) * slope_factor * channel_gain
    ).astype(bf16)
    weight_grad = weight_sum.reshape(taps, block, own) * (1.0 / math.sqrt(total_pixels))
    return (output, input_grad, weight_grad)


def solution(mesh):
    in_specs = (
        P(("groups", "tm"), "rows", None, "chan"),
        P("chan"),
        P(None, None, "chan"),
        P("groups"),
        P(("groups", "tm"), "rows", None, "chan"),
    )
    out_specs = (
        P(("groups", "tm"), "rows", None, "chan"),
        P(("groups", "tm"), "rows", None, "chan"),
        P("groups", ("tm", "rows"), "chan"),
    )
    return jax.shard_map(shards, mesh=mesh, in_specs=in_specs, out_specs=out_specs, check_vma=False)
```
